32 devices in a mesh: cfg: 2 (over y), seq: 16 (over z, x, core).
Axes of the slice: x: 2, y: 2, z: 4, core: 2. Of those that a mesh axis runs over, the one named last changes fastest.
Arguments:
- hidden: bfloat16 [2, 768, 3072], P('cfg', 'seq'), may hold values from -3 to 3
- queries: bfloat16 [2, 768, 2048], P('cfg', 'seq'), may hold values from -5 to 5
- key_proj: bfloat16 [2, 768, 2048], P('cfg', 'seq'), may hold values from -5 to 5
- value_proj: bfloat16 [2, 768, 2048], P('cfg', 'seq'), may hold values from -12 to 12
- norm_gain: float32 [2, 64], replicated, may hold values from 0.1 to 1.9
- norm_bias: float32 [2, 64], replicated, may hold values from -2 to 2
- positions: int32 [3, 768], P(None, 'seq'), may hold values from 0 to 47
- text_len: int32 [2], P('cfg'), may hold values from 1 to 226
- time_embed: bfloat16 [512], replicated, may hold values from -6 to 6
- gate_table: bfloat16 [512, 3072], P(None, 'seq'), may hold values from -0.25 to 0.25
- mod_table: bfloat16 [512, 6144], P(None, 'seq'), may hold values from -0.25 to 0.25
- out_weight: bfloat16 [2048, 3072], P(None, ('cfg', 'seq')), may hold values from -0.125 to 0.125
- proj_weight: bfloat16 [3072, 64], replicated, may hold values from -0.109375 to 0.109375
- proj_bias: float32 [64], replicated, may hold values from -3 to 3
- latent: float32 [768, 64], P('seq'), may hold values from -6 to 6
- solver_coef: float32 [2, 50], replicated, may hold values from 0.3 to 1.2
- step_index: int32 [1], replicated, may hold values from 0 to 49
Outputs:
- latent_next: float32 [768, 64], P('seq', 'cfg')
The draws below stay inside these ranges and needn't reach their ends.
All inputs are finite; a program needn't handle non-finite values.
Results may differ from the reference program's by a relative error of at most 0.0072.
Values may be sent and summed in bfloat16 or wider, within the bound.
A program may use at most 128 MiB of HBM per device.

```python
import math
import jax
import jax.numpy as jnp
import numpy as np
from jax import lax

D = 3072
HEADS = 32
HEAD_DIM = 64
TEMB = 512
CHANNELS = 64
TEXT = 226
TEXT_SLOTS = 256
STEPS = 50
TOKENS = 768


noise_level = 0.15


def slow_mask():
    table = np.zeros((64,), np.float32)
    for pair_index in [4, 5, 6, 7, 14, 15, 16, 17, 18, 19, 26, 27, 28, 29, 30, 31]:
        table[2 * pair_index] = 1.0
        table[2 * pair_index + 1] = 1.0
    return jnp.asarray(table)


def cluster_shared(key):
    group_count = max(TOKENS // 8, 1)
    cluster_ids = jax.random.randint(jax.random.fold_in(key, 11), (2, TOKENS, HEADS), 0, group_count)
    centres = jax.random.normal(jax.random.fold_in(key, 12), (2, group_count, HEADS, HEAD_DIM), jnp.float32)
    centres = jnp.clip(centres, -4.0, 4.0)
    half_index = jnp.arange(2)[:, None, None]
    head_index = jnp.arange(HEADS)[None, None, :]
    shared_part = centres[half_index, cluster_ids, head_index]
    return shared_part * slow_mask()[None, None, None, :]


def draw_queries(key, part):
    shared_part = cluster_shared(key)
    noise_key = jax.random.fold_in(key, 21)
    noise_part = jnp.clip(jax.random.normal(noise_key, shared_part.shape, jnp.float32), -4.0, 4.0)
    whole = shared_part + noise_level * noise_part
    return whole.reshape(2, TOKENS, HEADS * HEAD_DIM).astype(jnp.bfloat16)


def draw_key_proj(key, part):
    shared_part = cluster_shared(key)
    noise_key = jax.random.fold_in(key, 22)
    noise_part = jnp.clip(jax.random.normal(noise_key, shared_part.shape, jnp.float32), -4.0, 4.0)
    whole = shared_part + noise_level * noise_part
    return whole.reshape(2, TOKENS, HEADS * HEAD_DIM).astype(jnp.bfloat16)


def set_ends(result, key, least, largest):
    place = [jax.random.randint(jax.random.fold_in(key, axis), (), 0, length) for axis, length in enumerate(result.shape)]
    longest = result.shape.index(max(result.shape))
    beside = place[:longest] + [(place[longest] + 1) % result.shape[longest]] + place[longest + 1:]
    return result.at[tuple(place)].set(least).at[tuple(beside)].set(largest)


def level_of(own_key, dims, shards, smallest, top_value):
    loudness = 1.0
    for axis_at, shards_of in shards:
        steps = jax.random.uniform(jax.random.fold_in(jax.random.fold_in(own_key, 6), axis_at), (shards_of,), jnp.float32, smallest / len(shards), top_value / len(shards))
        loudness = loudness * jnp.repeat(jnp.exp(steps), dims[axis_at] // shards_of).reshape((-1,) + (1,) * (len(dims) - 1 - axis_at))
    return loudness


def noise(stream_key, extent, spread, most, shards=(), kind=jnp.bfloat16):
    gain = level_of(stream_key, extent, shards, -0.22, 0.18) if shards else 1.0
    drawn = jax.random.normal(stream_key, extent, jnp.float32) * spread * gain
    return jnp.minimum(jnp.maximum(drawn, -most), most).astype(kind)


def setup_inputs(seed: int = 0) -> dict:
    streams_of = jax.random.split(jax.random.key(seed), 18)
    return {
        "hidden": noise(streams_of[0], (2, TOKENS, D), 0.5, 3.0, ((0, 2), (1, 16))),
        "queries": draw_queries(jax.random.fold_in(streams_of[17], 71), 0),
        "key_proj": draw_key_proj(jax.random.fold_in(streams_of[17], 71), 0),
        "value_proj": noise(streams_of[3], (2, TOKENS, HEADS * HEAD_DIM), 2.0, 12.0, ((0, 2), (1, 16))),
        "norm_gain": jnp.clip(1.0 + 0.18 * jax.random.normal(streams_of[4], (2, HEAD_DIM), jnp.float32), 0.1, 1.9),
        "norm_bias": noise(streams_of[5], (2, HEAD_DIM), 0.3, 2.0, (), jnp.float32),
        "positions": set_ends(jax.random.randint(streams_of[6], (3, TOKENS), 0, 48), jax.random.fold_in(streams_of[6], 1), 0, 47).astype(jnp.int32),
        "text_len": jax.random.randint(streams_of[7], (2,), 1, TEXT + 1).astype(jnp.int32),
        "time_embed": noise(streams_of[8], (TEMB,), 1.0, 6.0),
        "gate_table": noise(streams_of[9], (TEMB, D), TEMB ** -0.5, 0.25, ((1, 16),)),
        "mod_table": noise(streams_of[10], (TEMB, 2 * D), TEMB ** -0.5, 0.25, ((1, 16),)),
        "out_weight": noise(streams_of[11], (HEADS * HEAD_DIM, D), (HEADS * HEAD_DIM) ** -0.5, 0.125, ((1, 32),)),
        "proj_weight": noise(streams_of[12], (D, CHANNELS), D ** -0.5, 0.109375),
        "proj_bias": noise(streams_of[13], (CHANNELS,), 0.5, 3.0, (), jnp.float32),
        "latent": noise(streams_of[14], (TOKENS, CHANNELS), 1.0, 6.0, ((0, 16),), jnp.float32),
        "solver_coef": jnp.clip(jax.random.uniform(streams_of[15], (2, STEPS), jnp.float32, 0.3, 1.2), 0.3, 1.2),
        "step_index": jax.random.randint(streams_of[16], (1,), 0, STEPS).astype(jnp.int32),
    }


GUIDANCE = 6.0

def layer_norm(values, epsilon):
    centre = lax.optimization_barrier(jnp.mean(values, axis=-1, keepdims=True))
    centred = values - centre
    variance = lax.optimization_barrier(jnp.mean(centred * centred, axis=-1, keepdims=True))
    return centred * lax.rsqrt(variance + epsilon)

def rotary_angles(positions):
    pos_float = positions.astype(jnp.float32)
    time_freq = jnp.asarray(10000.0 ** (-2.0 * np.arange(8) / 16.0), jnp.float32)
    space_freq = jnp.asarray(10000.0 ** (-2.0 * np.arange(12) / 24.0), jnp.float32)
    return jnp.concatenate([pos_float[0][:, None] * time_freq[None, :], pos_float[1][:, None] * space_freq[None, :], pos_float[2][:, None] * space_freq[None, :]], axis=1)

def norm_rotate(values, gain_row, offset, angles, is_video):
    row_count = values.shape[0]
    head_count = values.shape[1] // 64
    normed = layer_norm(values.astype(jnp.float32).reshape(row_count, head_count, 64), 1e-06) * gain_row + offset
    paired = normed.reshape(row_count, head_count, 32, 2)
    first_half = paired[..., 0]
    second = paired[..., 1]
    cosine = jnp.cos(angles)[:, None, :]
    sine_part = jnp.sin(angles)[:, None, :]
    rotated = jnp.stack([first_half * cosine - second * sine_part, first_half * sine_part + second * cosine], axis=-1).reshape(row_count, head_count, 64)
    return jnp.where(is_video[:, None, None], rotated, normed).astype(jnp.bfloat16)

def attend_head(head_query, head_key, head_value, key_valid):
    total_rows = head_query.shape[0]
    block_rows = math.gcd(1024, total_rows)

    def one_block(query_block):
        scores = jnp.dot(query_block, head_key.T, preferred_element_type=jnp.float32) * 0.125
        weights = jnp.where(key_valid[None, :], jnp.exp(scores), 0.0)
        denominator = lax.optimization_barrier(jnp.sum(weights, axis=1, keepdims=True))
        numerator = jnp.dot(weights.astype(jnp.bfloat16), head_value, preferred_element_type=jnp.float32)
        return (numerator / denominator).astype(jnp.bfloat16)
    return lax.map(one_block, head_query.reshape(total_rows // block_rows, block_rows, 64)).reshape(total_rows, 64)

def reference(hidden, queries, key_proj, value_proj, norm_gain, norm_bias, positions, text_len, time_embed, gate_table, mod_table, out_weight, proj_weight, proj_bias, latent, solver_coef, step_index):
    row_index = jnp.arange(TOKENS)
    is_video = row_index >= TEXT_SLOTS
    angles = rotary_angles(positions)
    embed_act = jax.nn.silu(time_embed.astype(jnp.float32)).astype(jnp.bfloat16)[None, :]
    gate_vec = jnp.dot(embed_act, gate_table, preferred_element_type=jnp.float32)[0]
    modulation = jnp.dot(embed_act, mod_table, preferred_element_type=jnp.float32)[0]
    shift_part = modulation[:D]
    scale_part = modulation[D:]
    predictions = []
    for half_index in range(2):
        rot_query = norm_rotate(queries[half_index], norm_gain[0], norm_bias[0], angles, is_video)
        rot_key = norm_rotate(key_proj[half_index], norm_gain[1], norm_bias[1], angles, is_video)
        key_valid = is_video | (row_index < text_len[half_index])
        head_values = value_proj[half_index].reshape(TOKENS, HEADS, 64)

        def per_head(operands):
            return attend_head(operands[0], operands[1], operands[2], key_valid)
        attended = lax.map(per_head, (rot_query.transpose(1, 0, 2), rot_key.transpose(1, 0, 2), head_values.transpose(1, 0, 2)))
        attended = attended.transpose(1, 0, 2).reshape(TOKENS, HEADS * 64)
        projected = jnp.dot(attended, out_weight, preferred_element_type=jnp.float32)
        residual = hidden[half_index].astype(jnp.float32) + gate_vec[None, :] * projected
        normed = (layer_norm(residual, 1e-05) * (1.0 + scale_part) + shift_part).astype(jnp.bfloat16)
        predictions.append(jnp.dot(normed, proj_weight, preferred_element_type=jnp.float32) + proj_bias)
    guided = predictions[1] + GUIDANCE * (predictions[0] - predictions[1])
    step_coefs = lax.dynamic_index_in_dim(solver_coef, step_index[0], axis=1, keepdims=False)
    updated = step_coefs[0] * latent + step_coefs[1] * guided
    return jnp.where(is_video[:, None], updated, 0.0)
```

```python
import math

import jax
import jax.numpy as jnp
import numpy as np
from jax import lax
from jax.sharding import PartitionSpec as P

TEXT_SLOTS = 256


GUIDANCE = 6.0


def swapped(value, axis, bit):
    return lax.ppermute(value, axis, [(i, i ^ 1 << bit) for i in range(lax.axis_size(axis))])


def layer_norm(values, epsilon):
    centre = jnp.mean(values, axis=-1, keepdims=True)
    centred = values - centre
    variance = jnp.mean(centred * centred, axis=-1, keepdims=True)
    return centred * lax.rsqrt(variance + epsilon)


def rotary_angles(positions):
    pos_float = positions.astype(jnp.float32)
    time_freq = jnp.asarray(10000.0 ** (-2.0 * np.arange(8) / 16.0), jnp.float32)
    space_freq = jnp.asarray(10000.0 ** (-2.0 * np.arange(12) / 24.0), jnp.float32)
    return jnp.concatenate(
        [
            pos_float[0][:, None] * time_freq[None, :],
            pos_float[1][:, None] * space_freq[None, :],
            pos_float[2][:, None] * space_freq[None, :],
        ],
        axis=1,
    )


def norm_rotate(values, gain_row, offset, angles, is_video):
    row_count = values.shape[0]
    head_count = values.shape[1] // 64
    normed = (
        layer_norm(values.astype(jnp.float32).reshape(row_count, head_count, 64), 1e-06) * gain_row
        + offset
    )
    paired = normed.reshape(row_count, head_count, 32, 2)
    first_half = paired[..., 0]
    second = paired[..., 1]
    cosine = jnp.cos(angles)[:, None, :]
    sine_part = jnp.sin(angles)[:, None, :]
    rotated = jnp.stack(
        [first_half * cosine - second * sine_part, first_half * sine_part + second * cosine],
        axis=-1,
    ).reshape(row_count, head_count, 64)
    return jnp.where(is_video[:, None, None], rotated, normed).astype(jnp.bfloat16)


def project_columns(attended, out_weight, seq_count, local_rows):
    head_group, query_count, _ = attended.shape
    own_width = out_weight.shape[1]
    partner_weight = swapped(out_weight, "cfg", 0)
    cfg_place = lax.axis_index("cfg")
    is_first = cfg_place == 0
    first = jnp.where(is_first, out_weight, partner_weight)
    second = jnp.where(is_first, partner_weight, out_weight)
    weights = jnp.concatenate([first, second], axis=1)
    own_heads = attended.transpose(1, 0, 2).reshape(query_count, head_group * 64)
    every = lax.all_gather(own_heads, "seq", axis=0)
    weights = weights.reshape(seq_count, head_group * 64, 2 * own_width)
    part = jnp.einsum("sqk,skn->qn", every, weights, preferred_element_type=jnp.float32)
    sent = part.astype(jnp.bfloat16).reshape(seq_count, local_rows * 2 * own_width)
    back = lax.all_to_all(sent, "seq", split_axis=0, concat_axis=0, tiled=True)
    back = back.reshape(seq_count, local_rows, 2, own_width).transpose(1, 2, 0, 3)
    return back.reshape(local_rows, 2 * seq_count * own_width).astype(jnp.float32)


def project_rows(attended, out_weight, seq_count, part_rows, row_split, head_sets):
    head_group = attended.shape[0]
    back_send = attended.reshape(head_group, seq_count, part_rows, 64).transpose(1, 2, 0, 3)
    back_send = back_send.reshape(seq_count, part_rows * head_group * 64)
    back_recv = lax.all_to_all(back_send, "seq", split_axis=0, concat_axis=0, tiled=True)
    attended_rows = back_recv.reshape(head_sets, row_split, part_rows, head_group, 64)
    attended_rows = attended_rows.transpose(1, 2, 0, 3, 4)
    attended_rows = attended_rows.reshape(row_split * part_rows, head_sets * head_group * 64)
    return jnp.dot(
        attended_rows,
        lax.all_gather(out_weight, ("cfg", "seq"), axis=1, tiled=True),
        preferred_element_type=jnp.float32,
    )


def on_device(
    hidden,
    queries,
    key_proj,
    value_proj,
    norm_gain,
    norm_bias,
    positions,
    text_len,
    time_embed,
    gate_table,
    mod_table,
    out_weight,
    proj_weight,
    proj_bias,
    latent,
    solver_coef,
    step_index,
):
    seq_count = lax.axis_size("seq")
    seq_place = lax.axis_index("seq")
    local_rows = queries.shape[1]
    head_count = queries.shape[2] // 64
    head_group = max(head_count // seq_count, 1)
    row_split = max(seq_count // head_count, 1)
    part_rows = local_rows // row_split
    head_sets = head_count // head_group
    row_index = seq_place * local_rows + jnp.arange(local_rows)
    is_video = row_index >= TEXT_SLOTS
    angles = rotary_angles(positions)
    rot_query = norm_rotate(queries[0], norm_gain[0], norm_bias[0], angles, is_video)
    rot_key = norm_rotate(key_proj[0], norm_gain[1], norm_bias[1], angles, is_video)
    query_send = rot_query.reshape(row_split, part_rows, head_sets, head_group, 64)
    query_send = query_send.transpose(2, 0, 1, 3, 4).reshape(seq_count, part_rows * head_group * 64)

    def spread(values):
        grouped = values.reshape(local_rows, head_sets, head_group * 64).transpose(1, 0, 2)
        widened = jnp.broadcast_to(
            grouped[:, None], (head_sets, row_split, local_rows, head_group * 64)
        )
        return widened.reshape(seq_count, local_rows * head_group * 64)

    key_send = spread(rot_key)
    value_send = spread(value_proj[0].reshape(local_rows, head_count, 64))
    query_recv, key_recv, value_recv = (
        lax.all_to_all(query_send, "seq", split_axis=0, concat_axis=0, tiled=True),
        lax.all_to_all(key_send, "seq", split_axis=0, concat_axis=0, tiled=True),
        lax.all_to_all(value_send, "seq", split_axis=0, concat_axis=0, tiled=True),
    )
    total_keys = seq_count * local_rows
    query_count = seq_count * part_rows
    query_all = query_recv.reshape(query_count, head_group, 64)
    key_index = jnp.arange(total_keys)
    key_valid = (key_index >= TEXT_SLOTS) | (key_index < text_len[0])
    block_keys = math.gcd(512, total_keys)
    block_count = total_keys // block_keys

    def key_step(state_pair, operands):
        numerator, denominator = state_pair
        key_block, value_block, valid_block = operands
        scores = (
            jnp.einsum("qgd,kgd->gqk", query_all, key_block, preferred_element_type=jnp.float32)
            * 0.125
        )
        weights = jnp.where(valid_block[None, None, :], jnp.exp(scores), 0.0)
        denominator = denominator + jnp.sum(weights, axis=2)
        numerator = numerator + jnp.einsum(
            "gqk,kgd->gqd",
            weights.astype(jnp.bfloat16),
            value_block,
            preferred_element_type=jnp.float32,
        )
        return ((numerator, denominator), None)

    start_state = (
        jnp.zeros((head_group, query_count, 64), jnp.float32),
        jnp.zeros((head_group, query_count), jnp.float32),
    )
    scanned = (
        key_recv.reshape(block_count, block_keys, head_group, 64),
        value_recv.reshape(block_count, block_keys, head_group, 64),
        key_valid.reshape(block_count, block_keys),
    )
    final_state, unused_out = lax.scan(key_step, start_state, scanned)
    attended = (final_state[0] / final_state[1][..., None]).astype(jnp.bfloat16)
    embed_act = jax.nn.silu(time_embed.astype(jnp.float32)).astype(jnp.bfloat16)[None, :]
    gate_own = jnp.dot(embed_act, gate_table, preferred_element_type=jnp.float32)
    mod_own = jnp.dot(embed_act, mod_table, preferred_element_type=jnp.float32)
    gate_width = gate_own.shape[1]
    vectors = lax.all_gather(jnp.concatenate([gate_own, mod_own], axis=1)[0], "seq", axis=0)
    gate_vec = vectors[:, :gate_width].reshape(-1)
    modulation = vectors[:, gate_width:].reshape(-1)
    if row_split == 1:
        projected = project_columns(attended, out_weight, seq_count, local_rows)
    else:
        projected = project_rows(attended, out_weight, seq_count, part_rows, row_split, head_sets)
    model_width = hidden.shape[2]
    residual = hidden[0].astype(jnp.float32) + gate_vec[None, :] * projected
    normed = (
        layer_norm(residual, 1e-05) * (1.0 + modulation[model_width:]) + modulation[:model_width]
    )
    normed = normed.astype(jnp.bfloat16)
    prediction = jnp.dot(normed, proj_weight, preferred_element_type=jnp.float32) + proj_bias
    cfg_place = lax.axis_index("cfg")
    own_width = prediction.shape[1] // 2
    own_pred = lax.dynamic_slice_in_dim(prediction, cfg_place * own_width, own_width, 1)
    sent_pred = lax.dynamic_slice_in_dim(prediction, (1 - cfg_place) * own_width, own_width, 1)
    partner = swapped(sent_pred, "cfg", 0)
    is_cond = cfg_place == 0
    cond_pred = jnp.where(is_cond, own_pred, partner)
    uncond_pred = jnp.where(is_cond, partner, own_pred)
    guided = uncond_pred + GUIDANCE * (cond_pred - uncond_pred)
    own_latent = lax.dynamic_slice_in_dim(latent, cfg_place * own_width, own_width, 1)
    step_coefs = lax.dynamic_index_in_dim(solver_coef, step_index[0], axis=1, keepdims=False)
    updated = step_coefs[0] * own_latent + step_coefs[1] * guided
    return jnp.where(is_video[:, None], updated, 0.0)


def solution(mesh):
    placed = (
        P("cfg", "seq", None),
        P("cfg", "seq", None),
        P("cfg", "seq", None),
        P("cfg", "seq", None),
        P(),
        P(),
        P(None, "seq"),
        P("cfg"),
        P(),
        P(None, "seq"),
        P(None, "seq"),
        P(None, ("cfg", "seq")),
        P(),
        P(),
        P("seq", None),
        P(),
        P(),
    )
    return jax.shard_map(
        on_device, mesh=mesh, in_specs=placed, out_specs=P("seq", "cfg"), check_vma=False
    )
```

```python
import functools
import math

import jax
import jax.numpy as jnp
import numpy as np
from jax import lax
from jax.experimental import pallas as pl
from jax.experimental.pallas import tpu as pltpu
from jax.sharding import PartitionSpec as P

TEXT_SLOTS = 256


GUIDANCE = 6.0


def swapped(value, axis, bit):
    return lax.ppermute(value, axis, [(i, i ^ 1 << bit) for i in range(lax.axis_size(axis))])


def layer_norm(values, epsilon):
    centre = jnp.mean(values, axis=-1, keepdims=True)
    centred = values - centre
    variance = jnp.mean(centred * centred, axis=-1, keepdims=True)
    return centred * lax.rsqrt(variance + epsilon)


def rotary_angles(positions):
    pos_float = positions.astype(jnp.float32)
    time_freq = jnp.asarray(10000.0 ** (-2.0 * np.arange(8) / 16.0), jnp.float32)
    space_freq = jnp.asarray(10000.0 ** (-2.0 * np.arange(12) / 24.0), jnp.float32)
    return jnp.concatenate(
        [
            pos_float[0][:, None] * time_freq[None, :],
            pos_float[1][:, None] * space_freq[None, :],
            pos_float[2][:, None] * space_freq[None, :],
        ],
        axis=1,
    )


def norm_rotate(values, gain_row, offset, angles, is_video):
    row_count = values.shape[0]
    head_count = values.shape[1] // 64
    normed = (
        layer_norm(values.astype(jnp.float32).reshape(row_count, head_count, 64), 1e-06) * gain_row
        + offset
    )
    paired = normed.reshape(row_count, head_count, 32, 2)
    first_half = paired[..., 0]
    second = paired[..., 1]
    cosine = jnp.cos(angles)[:, None, :]
    sine_part = jnp.sin(angles)[:, None, :]
    rotated = jnp.stack(
        [first_half * cosine - second * sine_part, first_half * sine_part + second * cosine],
        axis=-1,
    ).reshape(row_count, head_count, 64)
    return jnp.where(is_video[:, None, None], rotated, normed).astype(jnp.bfloat16)


def project_columns(attended, out_weight, seq_count, local_rows):
    head_group, query_count, _ = attended.shape
    own_width = out_weight.shape[1]
    partner_weight = swapped(out_weight, "cfg", 0)
    cfg_place = lax.axis_index("cfg")
    is_first = cfg_place == 0
    first = jnp.where(is_first, out_weight, partner_weight)
    second = jnp.where(is_first, partner_weight, out_weight)
    weights = jnp.concatenate([first, second], axis=1)
    own_heads = attended.transpose(1, 0, 2).reshape(query_count, head_group * 64)
    every = lax.all_gather(own_heads, "seq", axis=0)
    weights = weights.reshape(seq_count, head_group * 64, 2 * own_width)
    part = jnp.einsum("sqk,skn->qn", every, weights, preferred_element_type=jnp.float32)
    sent = part.astype(jnp.bfloat16).reshape(seq_count, local_rows * 2 * own_width)
    back = lax.all_to_all(sent, "seq", split_axis=0, concat_axis=0, tiled=True)
    back = back.reshape(seq_count, local_rows, 2, own_width).transpose(1, 2, 0, 3)
    return back.reshape(local_rows, 2 * seq_count * own_width).astype(jnp.float32)


def project_rows(attended, out_weight, seq_count, part_rows, row_split, head_sets):
    head_group = attended.shape[0]
    back_send = attended.reshape(head_group, seq_count, part_rows, 64).transpose(1, 2, 0, 3)
    back_send = back_send.reshape(seq_count, part_rows * head_group * 64)
    back_recv = lax.all_to_all(back_send, "seq", split_axis=0, concat_axis=0, tiled=True)
    attended_rows = back_recv.reshape(head_sets, row_split, part_rows, head_group, 64)
    attended_rows = attended_rows.transpose(1, 2, 0, 3, 4)
    attended_rows = attended_rows.reshape(row_split * part_rows, head_sets * head_group * 64)
    return jnp.dot(
        attended_rows,
        lax.all_gather(out_weight, ("cfg", "seq"), axis=1, tiled=True),
        preferred_element_type=jnp.float32,
    )


LANES = 128


def each(count, body, first=0):
    def step(index, carry):
        body(index)
        return carry

    lax.fori_loop(first, count, step, 0)


def dot32(left, right):
    return jnp.dot(left, right, preferred_element_type=jnp.float32)


def norm_turn(ref, gain, offset, cosine, sine_part, group_count, factor):
    rows = ref.shape[0]
    values = jnp.concatenate(
        [ref[:, g * LANES : (g + 1) * LANES] for g in range(group_count)], axis=0
    )
    down = lax.broadcasted_iota(jnp.int32, (LANES, LANES), 0) < 64
    across = lax.broadcasted_iota(jnp.int32, (LANES, LANES), 1) < 64
    average = jnp.where(down == across, 1.0 / 64, 0.0).astype(jnp.bfloat16)
    centred = values.astype(jnp.float32) - dot32(values, average)
    square = centred * centred
    high = square.astype(jnp.bfloat16)
    low = (square - high.astype(jnp.float32)).astype(jnp.bfloat16)
    variance = dot32(high, average) + dot32(low, average)
    normed = centred * lax.rsqrt(variance + 1e-06) * gain + offset
    even = lax.broadcasted_iota(jnp.int32, normed.shape, 1) % 2 == 0
    beside = jnp.where(even, -pltpu.roll(normed, LANES - 1, 1), pltpu.roll(normed, 1, 1))
    normed = normed.reshape(group_count, rows, LANES)
    beside = beside.reshape(group_count, rows, LANES)
    turned = normed * cosine[None] + beside * sine_part[None]
    return (turned * factor).astype(jnp.bfloat16)


def step_kernel(
    seq_count,
    text_len, step_index, solver_coef,
    hidden, queries, key_proj, value_proj, heads_norm, angles, time_embed, gate_table, mod_table,
    out_weight, proj_weight, proj_bias, latent,
    out,
    v_send, v_recv, qk_send, qk_recv, vec, partner_weight, every, part, back, total, gate_full,
    pred_send, pred_recv,
    v_sem, qk_sem, vec_sem, z_sem, x_sem, core_sem, back_sem, pair_sem,
):
    me = lax.axis_index("seq")
    cfg = lax.axis_index("cfg")
    layers = seq_count // 4
    layer, in_layer = me // 4, me % 4
    x_peer = me + 2 - 4 * ((me // 2) % 2)
    core_peer = me + 1 - 2 * (me % 2)
    rows = queries.shape[0]
    all_rows = seq_count * rows
    own_width = out_weight.shape[1]
    model_width = hidden.shape[1]

    barrier = pltpu.get_barrier_semaphore()

    def greet(d):
        pl.semaphore_signal(
            barrier, inc=1, device_id=(cfg, (me + d) % seq_count),
            device_id_type=pl.DeviceIdType.MESH,
        )

    each(seq_count, greet, 1)
    pl.semaphore_signal(
        barrier, inc=1, device_id=(1 - cfg, me), device_id_type=pl.DeviceIdType.MESH
    )
    for g in range(seq_count):
        v_send[g] = value_proj[:, g * LANES : (g + 1) * LANES]
    pl.semaphore_wait(barrier, seq_count)

    def remote(src, dst, sems, index, where):
        return pltpu.make_async_remote_copy(
            src_ref=src, dst_ref=dst, send_sem=sems.at[0, index], recv_sem=sems.at[1, index],
            device_id=where, device_id_type=pl.DeviceIdType.MESH,
        )

    def peer(d):
        return (me + d) % seq_count

    def v_copy(d):
        return remote(v_send.at[peer(d)], v_recv.at[me], v_sem, d, (cfg, peer(d)))

    def qk_copy(d):
        return remote(qk_send.at[peer(d)], qk_recv.at[me], qk_sem, d, (cfg, peer(d)))

    def vec_copy(d):
        return remote(vec.at[me], vec.at[me], vec_sem, d, (cfg, peer(d)))

    def back_copy(d):
        return remote(part.at[peer(d)], back.at[me], back_sem, d, (cfg, peer(d)))

    each(seq_count, lambda d: v_copy(d).start(), 1)
    weight_copy = remote(out_weight, partner_weight, pair_sem, 0, (1 - cfg, me))
    weight_copy.start()

    cosine = jnp.cos(angles[...])
    sine_part = jnp.sin(angles[...])
    qk_send[:, 1] = norm_turn(
        key_proj, heads_norm[1:2], heads_norm[3:4], cosine, sine_part, seq_count, 1.0
    )
    qk_send[:, 0] = norm_turn(
        queries, heads_norm[0:1], heads_norm[2:3], cosine, sine_part, seq_count, 0.125
    )
    each(seq_count, lambda d: qk_copy(d).start(), 1)
    v_recv[me] = v_send[me]
    qk_recv[me] = qk_send[me]

    embed = time_embed[...].astype(jnp.float32)
    embed = (embed * (1.0 / (1.0 + jnp.exp(-embed)))).astype(jnp.bfloat16)
    embed = jnp.broadcast_to(embed, (16, embed.shape[1]))
    gate_width = gate_table.shape[1]
    vec[me, :, 0:gate_width] = dot32(embed, gate_table[...])[0:1]
    vec[me, :, 256:] = dot32(embed, mod_table[...])[0:1]
    each(seq_count, lambda d: vec_copy(d).start(), 1)

    each(seq_count, lambda d: v_copy(d).wait(), 1)
    each(seq_count, lambda d: qk_copy(d).wait(), 1)

    keys = qk_recv[:, 1].reshape(all_rows, LANES)
    values = v_recv[...].reshape(all_rows, LANES)
    key_index = lax.broadcasted_iota(jnp.int32, (1, all_rows), 1)
    valid = (key_index >= TEXT_SLOTS) | (key_index < text_len[0])
    piece = 4

    def attend(index):
        asked = qk_recv[pl.ds(index * piece, piece), 0].reshape(piece * rows, LANES)
        lane = lax.broadcasted_iota(jnp.int32, asked.shape, 1)
        results = []
        for head in range(2):
            own = jnp.where((lane >= 64) == (head == 1), asked, jnp.zeros_like(asked))
            scores = lax.dot_general(
                own, keys, (((1,), (1,)), ((), ())), preferred_element_type=jnp.float32
            )
            weights = jnp.where(valid, jnp.exp(scores), 0.0)
            denominator = jnp.sum(weights, axis=1, keepdims=True)
            results.append(dot32(weights.astype(jnp.bfloat16), values) / denominator)
        both = jnp.where(lane < 64, results[0], results[1]).astype(jnp.bfloat16)
        start = pl.multiple_of(index * piece * rows, piece * rows)
        every[me, pl.ds(start, piece * rows), :] = both

    each(seq_count // piece, attend)

    def line(d):
        return (layer + layers - d) % layers * 4

    def z_copy(d):
        target = (layer + d) % layers * 4 + in_layer
        return remote(every.at[me], every.at[me], z_sem, d, (cfg, target))

    def x_copy(d):
        block = every.at[line(d) + in_layer]
        return remote(block, block, x_sem, d, (cfg, x_peer))

    def core_copy(d):
        block = every.at[line(d) + in_layer]
        return remote(block, block, core_sem, d, (cfg, core_peer))

    def cross_copy(d):
        block = every.at[line(d) + x_peer % 4]
        return remote(block, block, core_sem, layers + d, (cfg, core_peer))

    each(layers, lambda d: z_copy(layers - d).start(), 1)
    x_copy(0).start()
    core_copy(0).start()
    for d in range(layers):
        if d > 0:
            z_copy(d).wait_recv()
            x_copy(d).start()
            core_copy(d).start()
        if d > 0:
            x_copy(d - 1).wait_recv()
            cross_copy(d - 1).start()
    x_copy(layers - 1).wait_recv()
    cross_copy(layers - 1).start()
    weight_copy.wait()
    each(layers, lambda d: core_copy(d).wait_recv())
    each(layers, lambda d: cross_copy(d).wait_recv())

    def project(index):
        start = pl.multiple_of(index * piece * rows, piece * rows)
        asked = jnp.concatenate(
            [every[g, pl.ds(start, piece * rows), :] for g in range(seq_count)], axis=1
        )
        shape = (piece, rows, own_width)
        place = pl.ds(index * piece, piece)
        part[place, cfg] = dot32(asked, out_weight[...]).astype(jnp.bfloat16).reshape(shape)
        part[place, 1 - cfg] = (
            dot32(asked, partner_weight[...]).astype(jnp.bfloat16).reshape(shape)
        )

    each(seq_count // piece, project)
    each(seq_count, lambda d: back_copy(d).start(), 1)
    back[me] = part[me]
    each(seq_count, lambda d: vec_copy(d).wait(), 1)
    for g in range(seq_count):
        gate_full[:, g * gate_width : (g + 1) * gate_width] = vec[g, :, 0:gate_width]
    each(layers, lambda d: z_copy(d).wait_send(), 1)
    each(layers, lambda d: x_copy(d).wait_send())
    each(layers, lambda d: core_copy(d).wait_send())
    each(layers, lambda d: cross_copy(d).wait_send())
    each(seq_count, lambda d: back_copy(d).wait(), 1)

    for half in range(2):
        for g in range(seq_count):
            first = (half * seq_count + g) * own_width
            total[:, first : first + own_width] = back[g, half].astype(jnp.float32)
    residual = hidden[...].astype(jnp.float32) + gate_full[...] * total[...]
    centred = residual - jnp.mean(residual, axis=1, keepdims=True)
    variance = jnp.mean(centred * centred, axis=1, keepdims=True)
    normed = centred * lax.rsqrt(variance + 1e-05)
    half_count = seq_count // 2
    shift = jnp.concatenate([vec[g, :, 256:] for g in range(half_count)], axis=1)
    scale = jnp.concatenate([vec[half_count + g, :, 256:] for g in range(half_count)], axis=1)
    normed = (normed * (1.0 + scale) + shift).astype(jnp.bfloat16)
    prediction = dot32(normed, proj_weight[...]) + proj_bias[...]
    width = prediction.shape[1] // 2
    is_cond = cfg == 0
    left, right = prediction[:, :width], prediction[:, width:]
    own = jnp.where(is_cond, left, right)
    pred_send[...] = jnp.where(is_cond, right, left)
    pred_copy = remote(pred_send, pred_recv, pair_sem, 1, (1 - cfg, me))
    pred_copy.start()
    pred_copy.wait()
    other = pred_recv[...]
    cond = jnp.where(is_cond, own, other)
    uncond = jnp.where(is_cond, other, own)
    guided = uncond + GUIDANCE * (cond - uncond)
    own_latent = jnp.where(is_cond, latent[:, :width], latent[:, width:])
    at = step_index[0]
    updated = solver_coef[0, at] * own_latent + solver_coef[1, at] * guided
    row = me * rows + lax.broadcasted_iota(jnp.int32, updated.shape, 0)
    out[...] = jnp.where(row >= TEXT_SLOTS, updated, 0.0)


def in_one_kernel(
    hidden, queries, key_proj, value_proj, norm_gain, norm_bias, positions, text_len, time_embed,
    gate_table, mod_table, out_weight, proj_weight, proj_bias, latent, solver_coef, step_index,
):
    seq_count = lax.axis_size("seq")
    rows = queries.shape[1]
    row_index = lax.axis_index("seq") * rows + jnp.arange(rows)
    angles = jnp.where((row_index >= TEXT_SLOTS)[:, None], rotary_angles(positions), 0.0)
    angles = jnp.tile(jnp.repeat(angles, 2, axis=1), (1, 2))
    heads_norm = jnp.tile(jnp.concatenate([norm_gain, norm_bias], axis=0), (1, 2))
    own_width = out_weight.shape[1]
    model_width = hidden.shape[2]
    bf16, f32 = jnp.bfloat16, jnp.float32
    vec_width = 256 + mod_table.shape[1]
    out_width = latent.shape[1] // 2
    in_vmem = pl.BlockSpec(memory_space=pltpu.VMEM)
    in_smem = pl.BlockSpec(memory_space=pltpu.SMEM)

    def sems(count):
        return pltpu.SemaphoreType.DMA((2, count))

    return pl.pallas_call(
        functools.partial(step_kernel, seq_count),
        out_shape=jax.ShapeDtypeStruct((rows, out_width), f32),
        in_specs=[in_smem] * 3 + [in_vmem] * 13,
        out_specs=in_vmem,
        scratch_shapes=[
            pltpu.VMEM((seq_count, rows, LANES), bf16),
            pltpu.VMEM((seq_count, rows, LANES), bf16),
            pltpu.VMEM((seq_count, 2, rows, LANES), bf16),
            pltpu.VMEM((seq_count, 2, rows, LANES), bf16),
            pltpu.VMEM((seq_count, 1, vec_width), f32),
            pltpu.VMEM(out_weight.shape, bf16),
            pltpu.VMEM((seq_count, seq_count * rows, LANES), bf16),
            pltpu.VMEM((seq_count, 2, rows, own_width), bf16),
            pltpu.VMEM((seq_count, 2, rows, own_width), bf16),
            pltpu.VMEM((rows, model_width), f32),
            pltpu.VMEM((1, model_width), f32),
            pltpu.VMEM((rows, out_width), f32),
            pltpu.VMEM((rows, out_width), f32),
            sems(seq_count),
            sems(seq_count),
            sems(seq_count),
            sems(seq_count // 4),
            sems(seq_count // 4),
            sems(seq_count // 2),
            sems(seq_count),
            sems(2),
        ],
        compiler_params=pltpu.CompilerParams(
            collective_id=0, has_side_effects=True, vmem_limit_bytes=40 * 1024 * 1024
        ),
        name="sampling_step",
    )(
        text_len, step_index, solver_coef,
        hidden[0], queries[0], key_proj[0], value_proj[0], heads_norm, angles,
        time_embed[None, :], gate_table, mod_table, out_weight, proj_weight, proj_bias[None, :],
        latent,
    )


def on_device(
    hidden,
    queries,
    key_proj,
    value_proj,
    norm_gain,
    norm_bias,
    positions,
    text_len,
    time_embed,
    gate_table,
    mod_table,
    out_weight,
    proj_weight,
    proj_bias,
    latent,
    solver_coef,
    step_index,
):
    seq_count = lax.axis_size("seq")
    seq_place = lax.axis_index("seq")
    local_rows = queries.shape[1]
    head_count = queries.shape[2] // 64
    head_group = max(head_count // seq_count, 1)
    row_split = max(seq_count // head_count, 1)
    part_rows = local_rows // row_split
    head_sets = head_count // head_group
    if head_group * 64 == LANES and seq_count % 4 == 0 and local_rows % 16 == 0:
        return in_one_kernel(
            hidden, queries, key_proj, value_proj, norm_gain, norm_bias, positions, text_len,
            time_embed, gate_table, mod_table, out_weight, proj_weight, proj_bias, latent,
            solver_coef, step_index,
        )
    row_index = seq_place * local_rows + jnp.arange(local_rows)
    is_video = row_index >= TEXT_SLOTS
    angles = rotary_angles(positions)
    rot_query = norm_rotate(queries[0], norm_gain[0], norm_bias[0], angles, is_video)
    rot_key = norm_rotate(key_proj[0], norm_gain[1], norm_bias[1], angles, is_video)
    query_send = rot_query.reshape(row_split, part_rows, head_sets, head_group, 64)
    query_send = query_send.transpose(2, 0, 1, 3, 4).reshape(seq_count, part_rows * head_group * 64)

    def spread(values):
        grouped = values.reshape(local_rows, head_sets, head_group * 64).transpose(1, 0, 2)
        widened = jnp.broadcast_to(
            grouped[:, None], (head_sets, row_split, local_rows, head_group * 64)
        )
        return widened.reshape(seq_count, local_rows * head_group * 64)

    key_send = spread(rot_key)
    value_send = spread(value_proj[0].reshape(local_rows, head_count, 64))
    query_recv, key_recv, value_recv = (
        lax.all_to_all(query_send, "seq", split_axis=0, concat_axis=0, tiled=True),
        lax.all_to_all(key_send, "seq", split_axis=0, concat_axis=0, tiled=True),
        lax.all_to_all(value_send, "seq", split_axis=0, concat_axis=0, tiled=True),
    )
    total_keys = seq_count * local_rows
    query_count = seq_count * part_rows
    query_all = query_recv.reshape(query_count, head_group, 64)
    key_index = jnp.arange(total_keys)
    key_valid = (key_index >= TEXT_SLOTS) | (key_index < text_len[0])
    block_keys = math.gcd(512, total_keys)
    block_count = total_keys // block_keys

    def key_step(state_pair, operands):
        numerator, denominator = state_pair
        key_block, value_block, valid_block = operands
        scores = (
            jnp.einsum("qgd,kgd->gqk", query_all, key_block, preferred_element_type=jnp.float32)
            * 0.125
        )
        weights = jnp.where(valid_block[None, None, :], jnp.exp(scores), 0.0)
        denominator = denominator + jnp.sum(weights, axis=2)
        numerator = numerator + jnp.einsum(
            "gqk,kgd->gqd",
            weights.astype(jnp.bfloat16),
            value_block,
            preferred_element_type=jnp.float32,
        )
        return ((numerator, denominator), None)

    start_state = (
        jnp.zeros((head_group, query_count, 64), jnp.float32),
        jnp.zeros((head_group, query_count), jnp.float32),
    )
    scanned = (
        key_recv.reshape(block_count, block_keys, head_group, 64),
        value_recv.reshape(block_count, block_keys, head_group, 64),
        key_valid.reshape(block_count, block_keys),
    )
    final_state, unused_out = lax.scan(key_step, start_state, scanned)
    attended = (final_state[0] / final_state[1][..., None]).astype(jnp.bfloat16)
    embed_act = jax.nn.silu(time_embed.astype(jnp.float32)).astype(jnp.bfloat16)[None, :]
    gate_own = jnp.dot(embed_act, gate_table, preferred_element_type=jnp.float32)
    mod_own = jnp.dot(embed_act, mod_table, preferred_element_type=jnp.float32)
    gate_width = gate_own.shape[1]
    vectors = lax.all_gather(jnp.concatenate([gate_own, mod_own], axis=1)[0], "seq", axis=0)
    gate_vec = vectors[:, :gate_width].reshape(-1)
    modulation = vectors[:, gate_width:].reshape(-1)
    if row_split == 1:
        projected = project_columns(attended, out_weight, seq_count, local_rows)
    else:
        projected = project_rows(attended, out_weight, seq_count, part_rows, row_split, head_sets)
    model_width = hidden.shape[2]
    residual = hidden[0].astype(jnp.float32) + gate_vec[None, :] * projected
    normed = (
        layer_norm(residual, 1e-05) * (1.0 + modulation[model_width:]) + modulation[:model_width]
    )
    normed = normed.astype(jnp.bfloat16)
    prediction = jnp.dot(normed, proj_weight, preferred_element_type=jnp.float32) + proj_bias
    cfg_place = lax.axis_index("cfg")
    own_width = prediction.shape[1] // 2
    own_pred = lax.dynamic_slice_in_dim(prediction, cfg_place * own_width, own_width, 1)
    sent_pred = lax.dynamic_slice_in_dim(prediction, (1 - cfg_place) * own_width, own_width, 1)
    partner = swapped(sent_pred, "cfg", 0)
    is_cond = cfg_place == 0
    cond_pred = jnp.where(is_cond, own_pred, partner)
    uncond_pred = jnp.where(is_cond, partner, own_pred)
    guided = uncond_pred + GUIDANCE * (cond_pred - uncond_pred)
    own_latent = lax.dynamic_slice_in_dim(latent, cfg_place * own_width, own_width, 1)
    step_coefs = lax.dynamic_index_in_dim(solver_coef, step_index[0], axis=1, keepdims=False)
    updated = step_coefs[0] * own_latent + step_coefs[1] * guided
    return jnp.where(is_video[:, None], updated, 0.0)


def solution(mesh):
    placed = (
        P("cfg", "seq", None),
        P("cfg", "seq", None),
        P("cfg", "seq", None),
        P("cfg", "seq", None),
        P(),
        P(),
        P(None, "seq"),
        P("cfg"),
        P(),
        P(None, "seq"),
        P(None, "seq"),
        P(None, ("cfg", "seq")),
        P(),
        P(),
        P("seq", None),
        P(),
        P(),
    )
    return jax.shard_map(
        on_device, mesh=mesh, in_specs=placed, out_specs=P("seq", "cfg"), check_vma=False
    )
```

```python
import functools
import math

import jax
import jax.numpy as jnp
import numpy as np
from jax import lax
from jax.experimental import pallas as pl
from jax.experimental.pallas import tpu as pltpu
from jax.sharding import PartitionSpec as P

TEXT_SLOTS = 256


GUIDANCE = 6.0


def swapped(value, axis, bit):
    return lax.ppermute(value, axis, [(i, i ^ 1 << bit) for i in range(lax.axis_size(axis))])


def layer_norm(values, epsilon):
    centre = jnp.mean(values, axis=-1, keepdims=True)
    centred = values - centre
    variance = jnp.mean(centred * centred, axis=-1, keepdims=True)
    return centred * lax.rsqrt(variance + epsilon)


def rotary_angles(positions):
    pos_float = positions.astype(jnp.float32)
    time_freq = jnp.asarray(10000.0 ** (-2.0 * np.arange(8) / 16.0), jnp.float32)
    space_freq = jnp.asarray(10000.0 ** (-2.0 * np.arange(12) / 24.0), jnp.float32)
    return jnp.concatenate(
        [
            pos_float[0][:, None] * time_freq[None, :],
            pos_float[1][:, None] * space_freq[None, :],
            pos_float[2][:, None] * space_freq[None, :],
        ],
        axis=1,
    )


def norm_rotate(values, gain_row, offset, angles, is_video):
    row_count = values.shape[0]
    head_count = values.shape[1] // 64
    normed = (
        layer_norm(values.astype(jnp.float32).reshape(row_count, head_count, 64), 1e-06) * gain_row
        + offset
    )
    paired = normed.reshape(row_count, head_count, 32, 2)
    first_half = paired[..., 0]
    second = paired[..., 1]
    cosine = jnp.cos(angles)[:, None, :]
    sine_part = jnp.sin(angles)[:, None, :]
    rotated = jnp.stack(
        [first_half * cosine - second * sine_part, first_half * sine_part + second * cosine],
        axis=-1,
    ).reshape(row_count, head_count, 64)
    return jnp.where(is_video[:, None, None], rotated, normed).astype(jnp.bfloat16)


def project_columns(attended, out_weight, seq_count, local_rows):
    head_group, query_count, _ = attended.shape
    own_width = out_weight.shape[1]
    partner_weight = swapped(out_weight, "cfg", 0)
    cfg_place = lax.axis_index("cfg")
    is_first = cfg_place == 0
    first = jnp.where(is_first, out_weight, partner_weight)
    second = jnp.where(is_first, partner_weight, out_weight)
    weights = jnp.concatenate([first, second], axis=1)
    own_heads = attended.transpose(1, 0, 2).reshape(query_count, head_group * 64)
    every = lax.all_gather(own_heads, "seq", axis=0)
    weights = weights.reshape(seq_count, head_group * 64, 2 * own_width)
    part = jnp.einsum("sqk,skn->qn", every, weights, preferred_element_type=jnp.float32)
    sent = part.astype(jnp.bfloat16).reshape(seq_count, local_rows * 2 * own_width)
    back = lax.all_to_all(sent, "seq", split_axis=0, concat_axis=0, tiled=True)
    back = back.reshape(seq_count, local_rows, 2, own_width).transpose(1, 2, 0, 3)
    return back.reshape(local_rows, 2 * seq_count * own_width).astype(jnp.float32)


def project_rows(attended, out_weight, seq_count, part_rows, row_split, head_sets):
    head_group = attended.shape[0]
    back_send = attended.reshape(head_group, seq_count, part_rows, 64).transpose(1, 2, 0, 3)
    back_send = back_send.reshape(seq_count, part_rows * head_group * 64)
    back_recv = lax.all_to_all(back_send, "seq", split_axis=0, concat_axis=0, tiled=True)
    attended_rows = back_recv.reshape(head_sets, row_split, part_rows, head_group, 64)
    attended_rows = attended_rows.transpose(1, 2, 0, 3, 4)
    attended_rows = attended_rows.reshape(row_split * part_rows, head_sets * head_group * 64)
    return jnp.dot(
        attended_rows,
        lax.all_gather(out_weight, ("cfg", "seq"), axis=1, tiled=True),
        preferred_element_type=jnp.float32,
    )


LANES = 128


def each(count, body, first=0):
    def step(index, carry):
        body(index)
        return carry

    lax.fori_loop(first, count, step, 0)


def dot32(left, right):
    return jnp.dot(left, right, preferred_element_type=jnp.float32)


def dot_rows(left, right):
    return lax.dot_general(
        left, right, (((1,), (1,)), ((), ())), preferred_element_type=jnp.float32
    )


def norm_turn(ref, gain, offset, cosine, sine_part, group_count, factor):
    rows = ref.shape[0]
    values = jnp.concatenate(
        [ref[:, g * LANES : (g + 1) * LANES] for g in range(group_count)], axis=0
    )
    down = lax.broadcasted_iota(jnp.int32, (LANES, LANES), 0) < 64
    across = lax.broadcasted_iota(jnp.int32, (LANES, LANES), 1) < 64
    average = jnp.where(down == across, 1.0 / 64, 0.0).astype(jnp.bfloat16)
    centred = values.astype(jnp.float32) - dot32(values, average)
    square = centred * centred
    high = square.astype(jnp.bfloat16)
    low = (square - high.astype(jnp.float32)).astype(jnp.bfloat16)
    variance = dot32(high, average) + dot32(low, average)
    normed = centred * lax.rsqrt(variance + 1e-06) * gain + offset
    even = lax.broadcasted_iota(jnp.int32, normed.shape, 1) % 2 == 0
    beside = jnp.where(even, -pltpu.roll(normed, LANES - 1, 1), pltpu.roll(normed, 1, 1))
    normed = normed.reshape(group_count, rows, LANES)
    beside = beside.reshape(group_count, rows, LANES)
    turned = normed * cosine[None] + beside * sine_part[None]
    return (turned * factor).astype(jnp.bfloat16)


def step_kernel(
    seq_count,
    text_len, step_index, solver_coef,
    hidden, queries, key_proj, value_proj, norm_gain, norm_bias, positions, frequency, time_embed,
    gate_table, mod_table, out_weight, proj_weight, proj_bias, latent,
    out,
    v_send, v_recv, k_send, k_recv, q_send, q_recv, vec, partner_weight, every, part, back, total, gate_full,
    pred_send, pred_recv,
    v_sem, k_sem, q_sem, vec_sem, z_sem, x_sem, core_sem, back_sem, pair_sem,
):
    me = lax.axis_index("seq")
    cfg = lax.axis_index("cfg")
    layers = seq_count // 4
    layer, in_layer = me // 4, me % 4
    x_peer = me + 2 - 4 * ((me // 2) % 2)
    core_peer = me + 1 - 2 * (me % 2)
    rows = queries.shape[0]
    all_rows = seq_count * rows
    own_width = out_weight.shape[0]

    barrier = pltpu.get_barrier_semaphore()

    def greet(d):
        pl.semaphore_signal(
            barrier, inc=1, device_id=(cfg, (me + d) % seq_count),
            device_id_type=pl.DeviceIdType.MESH,
        )

    each(seq_count, greet, 1)
    pl.semaphore_signal(
        barrier, inc=1, device_id=(1 - cfg, me), device_id_type=pl.DeviceIdType.MESH
    )
    for g in range(seq_count):
        v_send[g] = value_proj[:, g * LANES : (g + 1) * LANES]
    lane = lax.broadcasted_iota(jnp.int32, (rows, LANES), 1)
    row = me * rows + lax.broadcasted_iota(jnp.int32, (rows, LANES), 0)
    pair = lane % 64
    place = jnp.where(
        pair < 16, positions[:, 0:1], jnp.where(pair < 40, positions[:, 1:2], positions[:, 2:3])
    )
    angles = jnp.where(row >= TEXT_SLOTS, place.astype(jnp.float32) * frequency[...], 0.0)
    cosine = jnp.cos(angles)
    sine_part = jnp.sin(angles)
    gain = jnp.concatenate([norm_gain[...], norm_gain[...]], axis=1)
    offset = jnp.concatenate([norm_bias[...], norm_bias[...]], axis=1)
    k_send[...] = norm_turn(
        key_proj, gain[1:2], offset[1:2], cosine, sine_part, seq_count, 1.0
    )
    pl.semaphore_wait(barrier, seq_count)

    def remote(src, dst, sems, index, where):
        return pltpu.make_async_remote_copy(
            src_ref=src, dst_ref=dst, send_sem=sems.at[0, index], recv_sem=sems.at[1, index],
            device_id=where, device_id_type=pl.DeviceIdType.MESH,
        )

    def peer(d):
        return (me + d) % seq_count

    def v_copy(d):
        return remote(v_send.at[peer(d)], v_recv.at[me], v_sem, d, (cfg, peer(d)))

    def k_copy(d):
        return remote(k_send.at[peer(d)], k_recv.at[me], k_sem, d, (cfg, peer(d)))

    def q_copy(d):
        return remote(q_send.at[peer(d)], q_recv.at[me], q_sem, d, (cfg, peer(d)))

    def vec_copy(d):
        return remote(vec.at[me], vec.at[me], vec_sem, d, (cfg, peer(d)))

    def back_copy(d):
        return remote(part.at[peer(d)], back.at[me], back_sem, d, (cfg, peer(d)))

    each(seq_count, lambda d: v_copy(d).start(), 1)
    each(seq_count, lambda d: k_copy(d).start(), 1)
    q_send[...] = norm_turn(
        queries, gain[0:1], offset[0:1], cosine, sine_part, seq_count, 0.125
    )
    each(seq_count, lambda d: q_copy(d).start(), 1)
    weight_copy = remote(out_weight, partner_weight, pair_sem, 0, (1 - cfg, me))
    weight_copy.start()
    v_recv[me] = v_send[me]
    k_recv[me] = k_send[me]
    q_recv[me] = q_send[me]

    embed = time_embed[...].astype(jnp.float32)
    embed = (embed * (1.0 / (1.0 + jnp.exp(-embed)))).astype(jnp.bfloat16)
    embed = jnp.broadcast_to(embed, (16, embed.shape[1]))
    gate_width = gate_table.shape[0]
    vec[me, :, 0:gate_width] = dot_rows(embed, gate_table[...])[0:1]
    vec[me, :, 256:] = dot32(embed, mod_table[...])[0:1]
    each(seq_count, lambda d: vec_copy(d).start(), 1)

    each(seq_count, lambda d: v_copy(d).wait(), 1)
    each(seq_count, lambda d: k_copy(d).wait(), 1)
    each(seq_count, lambda d: q_copy(d).wait(), 1)

    keys = k_recv[...].reshape(all_rows, LANES)
    values = v_recv[...].reshape(all_rows, LANES)
    key_index = lax.broadcasted_iota(jnp.int32, (1, all_rows), 1)
    valid = (key_index >= TEXT_SLOTS) | (key_index < text_len[0])

    def attend(piece):
        asked = jnp.concatenate([q_recv[4 * at + piece] for at in range(layers)], axis=0)
        lane = lax.broadcasted_iota(jnp.int32, asked.shape, 1)
        results = []
        for head in range(2):
            own = jnp.where((lane >= 64) == (head == 1), asked, jnp.zeros_like(asked))
            weights = jnp.where(valid, jnp.exp(dot_rows(own, keys)), 0.0)
            denominator = jnp.sum(weights, axis=1, keepdims=True)
            results.append(dot32(weights.astype(jnp.bfloat16), values) / denominator)
        every[me, piece] = jnp.where(lane < 64, results[0], results[1]).astype(jnp.bfloat16)

    def line(d):
        return (layer + layers - d) % layers * 4

    def z_copy(piece, d):
        target = (layer + d) % layers * 4 + in_layer
        block = every.at[me, piece]
        return remote(block, block, z_sem, piece * layers + d, (cfg, target))

    def x_copy(piece, d):
        block = every.at[line(d) + in_layer, piece]
        return remote(block, block, x_sem, piece * layers + d, (cfg, x_peer))

    def core_copy(piece, d):
        block = every.at[line(d) + in_layer, piece]
        return remote(block, block, core_sem, piece * layers + d, (cfg, core_peer))

    def cross_copy(piece, d):
        block = every.at[line(d) + x_peer % 4, piece]
        return remote(block, block, core_sem, (4 + piece) * layers + d, (cfg, core_peer))

    def give(piece):
        each(layers, lambda d: z_copy(piece, layers - d).start(), 1)
        x_copy(piece, 0).start()
        core_copy(piece, 0).start()

    def forward(piece):
        def from_line(d):
            z_copy(piece, d).wait_recv()
            x_copy(piece, d).start()
            core_copy(piece, d).start()
            x_copy(piece, d - 1).wait_recv()
            cross_copy(piece, d - 1).start()

        each(layers, from_line, 1)
        x_copy(piece, layers - 1).wait_recv()
        cross_copy(piece, layers - 1).start()

    def project(piece):
        each(layers, lambda d: core_copy(piece, d).wait_recv())
        each(layers, lambda d: cross_copy(piece, d).wait_recv())
        asked = jnp.concatenate([every[g, piece] for g in range(seq_count)], axis=1)
        shape = (layers, rows, own_width)
        own = dot_rows(asked, out_weight[...]).astype(jnp.bfloat16).reshape(shape)
        other = dot_rows(asked, partner_weight[...]).astype(jnp.bfloat16).reshape(shape)
        for at in range(layers):
            part[4 * at + piece, cfg] = own[at]
            part[4 * at + piece, 1 - cfg] = other[at]

        def hand_back(at):
            d = (4 * at + piece + seq_count - me) % seq_count

            @pl.when(d != 0)
            def _():
                back_copy(d).start()

        each(layers, hand_back)

    attend(0)
    give(0)
    attend(1)
    give(1)
    attend(2)
    give(2)
    forward(0)
    attend(3)
    give(3)
    forward(1)
    weight_copy.wait()
    forward(2)
    project(0)
    forward(3)
    project(1)
    project(2)
    project(3)
    back[me] = part[me]
    each(seq_count, lambda d: vec_copy(d).wait(), 1)
    for g in range(seq_count):
        gate_full[:, g * gate_width : (g + 1) * gate_width] = vec[g, :, 0:gate_width]
    for piece in range(4):
        each(layers, lambda d: z_copy(piece, d).wait_send(), 1)
        each(layers, lambda d: x_copy(piece, d).wait_send())
        each(layers, lambda d: core_copy(piece, d).wait_send())
        each(layers, lambda d: cross_copy(piece, d).wait_send())
    each(seq_count, lambda d: back_copy(d).wait(), 1)

    for half in range(2):
        for g in range(seq_count):
            first = (half * seq_count + g) * own_width
            total[:, first : first + own_width] = back[g, half].astype(jnp.float32)
    residual = hidden[...].astype(jnp.float32) + gate_full[...] * total[...]
    centred = residual - jnp.mean(residual, axis=1, keepdims=True)
    variance = jnp.mean(centred * centred, axis=1, keepdims=True)
    normed = centred * lax.rsqrt(variance + 1e-05)
    half_count = seq_count // 2
    shift = jnp.concatenate([vec[g, :, 256:] for g in range(half_count)], axis=1)
    scale = jnp.concatenate([vec[half_count + g, :, 256:] for g in range(half_count)], axis=1)
    normed = (normed * (1.0 + scale) + shift).astype(jnp.bfloat16)
    prediction = dot_rows(normed, proj_weight[...]) + proj_bias[...]
    width = prediction.shape[1] // 2
    is_cond = cfg == 0
    left, right = prediction[:, :width], prediction[:, width:]
    own = jnp.where(is_cond, left, right)
    pred_send[...] = jnp.where(is_cond, right, left)
    pred_copy = remote(pred_send, pred_recv, pair_sem, 1, (1 - cfg, me))
    pred_copy.start()
    pred_copy.wait()
    other = pred_recv[...]
    cond = jnp.where(is_cond, own, other)
    uncond = jnp.where(is_cond, other, own)
    guided = uncond + GUIDANCE * (cond - uncond)
    own_latent = jnp.where(is_cond, latent[:, :width], latent[:, width:])
    at = step_index[0]
    updated = solver_coef[0, at] * own_latent + solver_coef[1, at] * guided
    out_row = me * rows + lax.broadcasted_iota(jnp.int32, updated.shape, 0)
    out[...] = jnp.where(out_row >= TEXT_SLOTS, updated, 0.0)


def in_one_kernel(
    hidden, queries, key_proj, value_proj, norm_gain, norm_bias, positions, text_len, time_embed,
    gate_table, mod_table, out_weight, proj_weight, proj_bias, latent, solver_coef, step_index,
):
    seq_count = lax.axis_size("seq")
    rows = queries.shape[1]
    time_freq = 10000.0 ** (-2.0 * np.arange(8) / 16.0)
    space_freq = 10000.0 ** (-2.0 * np.arange(12) / 24.0)
    frequency = np.repeat(np.concatenate([time_freq, space_freq, space_freq]), 2)
    frequency = np.tile(frequency, 2).astype(np.float32)[None, :]
    own_width = out_weight.shape[1]
    model_width = hidden.shape[2]
    bf16, f32 = jnp.bfloat16, jnp.float32
    vec_width = 256 + mod_table.shape[1]
    out_width = latent.shape[1] // 2
    in_vmem = pl.BlockSpec(memory_space=pltpu.VMEM)
    in_smem = pl.BlockSpec(memory_space=pltpu.SMEM)

    def sems(count):
        return pltpu.SemaphoreType.DMA((2, count))

    return pl.pallas_call(
        functools.partial(step_kernel, seq_count),
        out_shape=jax.ShapeDtypeStruct((rows, out_width), f32),
        in_specs=[in_smem] * 3 + [in_vmem] * 15,
        out_specs=in_vmem,
        scratch_shapes=[
            pltpu.VMEM((seq_count, rows, LANES), bf16),
            pltpu.VMEM((seq_count, rows, LANES), bf16),
            pltpu.VMEM((seq_count, rows, LANES), bf16),
            pltpu.VMEM((seq_count, rows, LANES), bf16),
            pltpu.VMEM((seq_count, rows, LANES), bf16),
            pltpu.VMEM((seq_count, rows, LANES), bf16),
            pltpu.VMEM((seq_count, 1, vec_width), f32),
            pltpu.VMEM(out_weight.shape[::-1], bf16),
            pltpu.VMEM((seq_count, 4, seq_count // 4 * rows, LANES), bf16),
            pltpu.VMEM((seq_count, 2, rows, own_width), bf16),
            pltpu.VMEM((seq_count, 2, rows, own_width), bf16),
            pltpu.VMEM((rows, model_width), f32),
            pltpu.VMEM((1, model_width), f32),
            pltpu.VMEM((rows, out_width), f32),
            pltpu.VMEM((rows, out_width), f32),
            sems(seq_count),
            sems(seq_count),
            sems(seq_count),
            sems(seq_count),
            sems(seq_count),
            sems(seq_count),
            sems(seq_count * 2),
            sems(seq_count),
            sems(2),
        ],
        compiler_params=pltpu.CompilerParams(
            collective_id=0, has_side_effects=True, vmem_limit_bytes=40 * 1024 * 1024
        ),
        name="sampling_step",
    )(
        text_len, step_index, solver_coef,
        hidden[0], queries[0], key_proj[0], value_proj[0], norm_gain, norm_bias, positions.T,
        frequency, time_embed[None, :], gate_table.T, mod_table, out_weight.T, proj_weight.T,
        proj_bias[None, :],
        latent,
    )


def on_device(
    hidden,
    queries,
    key_proj,
    value_proj,
    norm_gain,
    norm_bias,
    positions,
    text_len,
    time_embed,
    gate_table,
    mod_table,
    out_weight,
    proj_weight,
    proj_bias,
    latent,
    solver_coef,
    step_index,
):
    seq_count = lax.axis_size("seq")
    seq_place = lax.axis_index("seq")
    local_rows = queries.shape[1]
    head_count = queries.shape[2] // 64
    head_group = max(head_count // seq_count, 1)
    row_split = max(seq_count // head_count, 1)
    part_rows = local_rows // row_split
    head_sets = head_count // head_group
    if head_group * 64 == LANES and seq_count % 4 == 0 and local_rows % 16 == 0:
        return in_one_kernel(
            hidden, queries, key_proj, value_proj, norm_gain, norm_bias, positions, text_len,
            time_embed, gate_table, mod_table, out_weight, proj_weight, proj_bias, latent,
            solver_coef, step_index,
        )
    row_index = seq_place * local_rows + jnp.arange(local_rows)
    is_video = row_index >= TEXT_SLOTS
    angles = rotary_angles(positions)
    rot_query = norm_rotate(queries[0], norm_gain[0], norm_bias[0], angles, is_video)
    rot_key = norm_rotate(key_proj[0], norm_gain[1], norm_bias[1], angles, is_video)
    query_send = rot_query.reshape(row_split, part_rows, head_sets, head_group, 64)
    query_send = query_send.transpose(2, 0, 1, 3, 4).reshape(seq_count, part_rows * head_group * 64)

    def spread(values):
        grouped = values.reshape(local_rows, head_sets, head_group * 64).transpose(1, 0, 2)
        widened = jnp.broadcast_to(
            grouped[:, None], (head_sets, row_split, local_rows, head_group * 64)
        )
        return widened.reshape(seq_count, local_rows * head_group * 64)

    key_send = spread(rot_key)
    value_send = spread(value_proj[0].reshape(local_rows, head_count, 64))
    query_recv, key_recv, value_recv = (
        lax.all_to_all(query_send, "seq", split_axis=0, concat_axis=0, tiled=True),
        lax.all_to_all(key_send, "seq", split_axis=0, concat_axis=0, tiled=True),
        lax.all_to_all(value_send, "seq", split_axis=0, concat_axis=0, tiled=True),
    )
    total_keys = seq_count * local_rows
    query_count = seq_count * part_rows
    query_all = query_recv.reshape(query_count, head_group, 64)
    key_index = jnp.arange(total_keys)
    key_valid = (key_index >= TEXT_SLOTS) | (key_index < text_len[0])
    block_keys = math.gcd(512, total_keys)
    block_count = total_keys // block_keys

    def key_step(state_pair, operands):
        numerator, denominator = state_pair
        key_block, value_block, valid_block = operands
        scores = (
            jnp.einsum("qgd,kgd->gqk", query_all, key_block, preferred_element_type=jnp.float32)
            * 0.125
        )
        weights = jnp.where(valid_block[None, None, :], jnp.exp(scores), 0.0)
        denominator = denominator + jnp.sum(weights, axis=2)
        numerator = numerator + jnp.einsum(
            "gqk,kgd->gqd",
            weights.astype(jnp.bfloat16),
            value_block,
            preferred_element_type=jnp.float32,
        )
        return ((numerator, denominator), None)

    start_state = (
        jnp.zeros((head_group, query_count, 64), jnp.float32),
        jnp.zeros((head_group, query_count), jnp.float32),
    )
    scanned = (
        key_recv.reshape(block_count, block_keys, head_group, 64),
        value_recv.reshape(block_count, block_keys, head_group, 64),
        key_valid.reshape(block_count, block_keys),
    )
    final_state, unused_out = lax.scan(key_step, start_state, scanned)
    attended = (final_state[0] / final_state[1][..., None]).astype(jnp.bfloat16)
    embed_act = jax.nn.silu(time_embed.astype(jnp.float32)).astype(jnp.bfloat16)[None, :]
    gate_own = jnp.dot(embed_act, gate_table, preferred_element_type=jnp.float32)
    mod_own = jnp.dot(embed_act, mod_table, preferred_element_type=jnp.float32)
    gate_width = gate_own.shape[1]
    vectors = lax.all_gather(jnp.concatenate([gate_own, mod_own], axis=1)[0], "seq", axis=0)
    gate_vec = vectors[:, :gate_width].reshape(-1)
    modulation = vectors[:, gate_width:].reshape(-1)
    if row_split == 1:
        projected = project_columns(attended, out_weight, seq_count, local_rows)
    else:
        projected = project_rows(attended, out_weight, seq_count, part_rows, row_split, head_sets)
    model_width = hidden.shape[2]
    residual = hidden[0].astype(jnp.float32) + gate_vec[None, :] * projected
    normed = (
        layer_norm(residual, 1e-05) * (1.0 + modulation[model_width:]) + modulation[:model_width]
    )
    normed = normed.astype(jnp.bfloat16)
    prediction = jnp.dot(normed, proj_weight, preferred_element_type=jnp.float32) + proj_bias
    cfg_place = lax.axis_index("cfg")
    own_width = prediction.shape[1] // 2
    own_pred = lax.dynamic_slice_in_dim(prediction, cfg_place * own_width, own_width, 1)
    sent_pred = lax.dynamic_slice_in_dim(prediction, (1 - cfg_place) * own_width, own_width, 1)
    partner = swapped(sent_pred, "cfg", 0)
    is_cond = cfg_place == 0
    cond_pred = jnp.where(is_cond, own_pred, partner)
    uncond_pred = jnp.where(is_cond, partner, own_pred)
    guided = uncond_pred + GUIDANCE * (cond_pred - uncond_pred)
    own_latent = lax.dynamic_slice_in_dim(latent, cfg_place * own_width, own_width, 1)
    step_coefs = lax.dynamic_index_in_dim(solver_coef, step_index[0], axis=1, keepdims=False)
    updated = step_coefs[0] * own_latent + step_coefs[1] * guided
    return jnp.where(is_video[:, None], updated, 0.0)


def solution(mesh):
    placed = (
        P("cfg", "seq", None),
        P("cfg", "seq", None),
        P("cfg", "seq", None),
        P("cfg", "seq", None),
        P(),
        P(),
        P(None, "seq"),
        P("cfg"),
        P(),
        P(None, "seq"),
        P(None, "seq"),
        P(None, ("cfg", "seq")),
        P(),
        P(),
        P("seq", None),
        P(),
        P(),
    )
    return jax.shard_map(
        on_device, mesh=mesh, in_specs=placed, out_specs=P("seq", "cfg"), check_vma=False
    )
```

```python
import functools
import math

import jax
import jax.numpy as jnp
import numpy as np
from jax import lax
from jax.experimental import pallas as pl
from jax.experimental.pallas import tpu as pltpu
from jax.sharding import PartitionSpec as P

TEXT_SLOTS = 256


GUIDANCE = 6.0


def swapped(value, axis, bit):
    return lax.ppermute(value, axis, [(i, i ^ 1 << bit) for i in range(lax.axis_size(axis))])


def layer_norm(values, epsilon):
    centre = jnp.mean(values, axis=-1, keepdims=True)
    centred = values - centre
    variance = jnp.mean(centred * centred, axis=-1, keepdims=True)
    return centred * lax.rsqrt(variance + epsilon)


def rotary_angles(positions):
    pos_float = positions.astype(jnp.float32)
    time_freq = jnp.asarray(10000.0 ** (-2.0 * np.arange(8) / 16.0), jnp.float32)
    space_freq = jnp.asarray(10000.0 ** (-2.0 * np.arange(12) / 24.0), jnp.float32)
    return jnp.concatenate(
        [
            pos_float[0][:, None] * time_freq[None, :],
            pos_float[1][:, None] * space_freq[None, :],
            pos_float[2][:, None] * space_freq[None, :],
        ],
        axis=1,
    )


def norm_rotate(values, gain_row, offset, angles, is_video):
    row_count = values.shape[0]
    head_count = values.shape[1] // 64
    normed = (
        layer_norm(values.astype(jnp.float32).reshape(row_count, head_count, 64), 1e-06) * gain_row
        + offset
    )
    paired = normed.reshape(row_count, head_count, 32, 2)
    first_half = paired[..., 0]
    second = paired[..., 1]
    cosine = jnp.cos(angles)[:, None, :]
    sine_part = jnp.sin(angles)[:, None, :]
    rotated = jnp.stack(
        [first_half * cosine - second * sine_part, first_half * sine_part + second * cosine],
        axis=-1,
    ).reshape(row_count, head_count, 64)
    return jnp.where(is_video[:, None, None], rotated, normed).astype(jnp.bfloat16)


def project_columns(attended, out_weight, seq_count, local_rows):
    head_group, query_count, _ = attended.shape
    own_width = out_weight.shape[1]
    partner_weight = swapped(out_weight, "cfg", 0)
    cfg_place = lax.axis_index("cfg")
    is_first = cfg_place == 0
    first = jnp.where(is_first, out_weight, partner_weight)
    second = jnp.where(is_first, partner_weight, out_weight)
    weights = jnp.concatenate([first, second], axis=1)
    own_heads = attended.transpose(1, 0, 2).reshape(query_count, head_group * 64)
    every = lax.all_gather(own_heads, "seq", axis=0)
    weights = weights.reshape(seq_count, head_group * 64, 2 * own_width)
    part = jnp.einsum("sqk,skn->qn", every, weights, preferred_element_type=jnp.float32)
    sent = part.astype(jnp.bfloat16).reshape(seq_count, local_rows * 2 * own_width)
    back = lax.all_to_all(sent, "seq", split_axis=0, concat_axis=0, tiled=True)
    back = back.reshape(seq_count, local_rows, 2, own_width).transpose(1, 2, 0, 3)
    return back.reshape(local_rows, 2 * seq_count * own_width).astype(jnp.float32)


def project_rows(attended, out_weight, seq_count, part_rows, row_split, head_sets):
    head_group = attended.shape[0]
    back_send = attended.reshape(head_group, seq_count, part_rows, 64).transpose(1, 2, 0, 3)
    back_send = back_send.reshape(seq_count, part_rows * head_group * 64)
    back_recv = lax.all_to_all(back_send, "seq", split_axis=0, concat_axis=0, tiled=True)
    attended_rows = back_recv.reshape(head_sets, row_split, part_rows, head_group, 64)
    attended_rows = attended_rows.transpose(1, 2, 0, 3, 4)
    attended_rows = attended_rows.reshape(row_split * part_rows, head_sets * head_group * 64)
    return jnp.dot(
        attended_rows,
        lax.all_gather(out_weight, ("cfg", "seq"), axis=1, tiled=True),
        preferred_element_type=jnp.float32,
    )


LANES = 128


def each(count, body, first=0):
    def step(index, carry):
        body(index)
        return carry

    lax.fori_loop(first, count, step, 0)


def dot32(left, right):
    return jnp.dot(left, right, preferred_element_type=jnp.float32)


def dot_rows(left, right):
    return lax.dot_general(
        left, right, (((1,), (1,)), ((), ())), preferred_element_type=jnp.float32
    )


def norm_turn(ref, gain, offset, cosine, sine_part, group_count, factor):
    rows = ref.shape[0]
    values = jnp.concatenate(
        [ref[:, g * LANES : (g + 1) * LANES] for g in range(group_count)], axis=0
    )
    down = lax.broadcasted_iota(jnp.int32, (LANES, LANES), 0) < 64
    across = lax.broadcasted_iota(jnp.int32, (LANES, LANES), 1) < 64
    average = jnp.where(down == across, 1.0 / 64, 0.0).astype(jnp.bfloat16)
    centred = values.astype(jnp.float32) - dot32(values, average)
    square = centred * centred
    high = square.astype(jnp.bfloat16)
    low = (square - high.astype(jnp.float32)).astype(jnp.bfloat16)
    variance = dot32(high, average) + dot32(low, average)
    normed = centred * lax.rsqrt(variance + 1e-06) * gain + offset
    even = lax.broadcasted_iota(jnp.int32, normed.shape, 1) % 2 == 0
    beside = jnp.where(even, -pltpu.roll(normed, LANES - 1, 1), pltpu.roll(normed, 1, 1))
    normed = normed.reshape(group_count, rows, LANES)
    beside = beside.reshape(group_count, rows, LANES)
    turned = normed * cosine[None] + beside * sine_part[None]
    return (turned * factor).astype(jnp.bfloat16)


def step_kernel(
    seq_count,
    text_len, step_index, solver_coef,
    norm_gain, norm_bias, positions, frequency, time_embed, proj_bias,
    value_far, key_far, query_far, gate_far, mod_far, out_far, hidden_far, proj_far, latent_far,
    out,
    value_proj, key_proj, queries, gate_table, mod_table, out_weight, hidden, proj_weight, latent,
    load_sem,
    v_send, v_recv, k_send, k_recv, q_send, q_recv, vec, partner_weight, every, part, back, total, gate_full,
    pred_send, pred_recv,
    v_sem, k_sem, q_sem, vec_sem, z_sem, x_sem, core_sem, back_sem, pair_sem,
):
    me = lax.axis_index("seq")
    cfg = lax.axis_index("cfg")
    layers = seq_count // 4
    layer, in_layer = me // 4, me % 4
    x_peer = me + 2 - 4 * ((me // 2) % 2)
    core_peer = me + 1 - 2 * (me % 2)
    rows = queries.shape[0]
    all_rows = seq_count * rows
    own_width = out_weight.shape[0]

    loads = [
        pltpu.make_async_copy(far, near, load_sem.at[index])
        for index, (far, near) in enumerate(
            [
                (value_far, value_proj),
                (key_far, key_proj),
                (query_far, queries),
                (gate_far, gate_table),
                (mod_far, mod_table),
                (out_far, out_weight),
                (hidden_far, hidden),
                (proj_far, proj_weight),
                (latent_far, latent),
            ]
        )
    ]
    for load in loads:
        load.start()

    barrier = pltpu.get_barrier_semaphore()

    def greet(d):
        pl.semaphore_signal(
            barrier, inc=1, device_id=(cfg, (me + d) % seq_count),
            device_id_type=pl.DeviceIdType.MESH,
        )

    each(seq_count, greet, 1)
    pl.semaphore_signal(
        barrier, inc=1, device_id=(1 - cfg, me), device_id_type=pl.DeviceIdType.MESH
    )
    loads[0].wait()
    for g in range(seq_count):
        v_send[g] = value_proj[:, g * LANES : (g + 1) * LANES]
    lane = lax.broadcasted_iota(jnp.int32, (rows, LANES), 1)
    row = me * rows + lax.broadcasted_iota(jnp.int32, (rows, LANES), 0)
    pair = lane % 64
    place = jnp.where(
        pair < 16, positions[:, 0:1], jnp.where(pair < 40, positions[:, 1:2], positions[:, 2:3])
    )
    angles = jnp.where(row >= TEXT_SLOTS, place.astype(jnp.float32) * frequency[...], 0.0)
    cosine = jnp.cos(angles)
    sine_part = jnp.sin(angles)
    gain = jnp.concatenate([norm_gain[...], norm_gain[...]], axis=1)
    offset = jnp.concatenate([norm_bias[...], norm_bias[...]], axis=1)
    loads[1].wait()
    k_send[...] = norm_turn(
        key_proj, gain[1:2], offset[1:2], cosine, sine_part, seq_count, 1.0
    )
    pl.semaphore_wait(barrier, seq_count)

    def remote(src, dst, sems, index, where):
        return pltpu.make_async_remote_copy(
            src_ref=src, dst_ref=dst, send_sem=sems.at[0, index], recv_sem=sems.at[1, index],
            device_id=where, device_id_type=pl.DeviceIdType.MESH,
        )

    def peer(d):
        return (me + d) % seq_count

    def v_copy(d):
        return remote(v_send.at[peer(d)], v_recv.at[me], v_sem, d, (cfg, peer(d)))

    def k_copy(d):
        return remote(k_send.at[peer(d)], k_recv.at[me], k_sem, d, (cfg, peer(d)))

    def q_copy(d):
        return remote(q_send.at[peer(d)], q_recv.at[me], q_sem, d, (cfg, peer(d)))

    def vec_copy(d):
        return remote(vec.at[me], vec.at[me], vec_sem, d, (cfg, peer(d)))

    def back_copy(d):
        return remote(part.at[peer(d)], back.at[me], back_sem, d, (cfg, peer(d)))

    each(seq_count, lambda d: v_copy(d).start(), 1)
    each(seq_count, lambda d: k_copy(d).start(), 1)
    loads[2].wait()
    q_send[...] = norm_turn(
        queries, gain[0:1], offset[0:1], cosine, sine_part, seq_count, 0.125
    )
    each(seq_count, lambda d: q_copy(d).start(), 1)
    for load in loads[3:]:
        load.wait()
    weight_copy = remote(out_weight, partner_weight, pair_sem, 0, (1 - cfg, me))
    weight_copy.start()
    v_recv[me] = v_send[me]
    k_recv[me] = k_send[me]
    q_recv[me] = q_send[me]

    embed = time_embed[...].astype(jnp.float32)
    embed = (embed * (1.0 / (1.0 + jnp.exp(-embed)))).astype(jnp.bfloat16)
    embed = jnp.broadcast_to(embed, (16, embed.shape[1]))
    gate_width = gate_table.shape[0]
    vec[me, :, 0:gate_width] = dot_rows(embed, gate_table[...])[0:1]
    vec[me, :, 256:] = dot32(embed, mod_table[...])[0:1]
    each(seq_count, lambda d: vec_copy(d).start(), 1)

    each(seq_count, lambda d: v_copy(d).wait(), 1)
    each(seq_count, lambda d: k_copy(d).wait(), 1)
    each(seq_count, lambda d: q_copy(d).wait(), 1)

    keys = k_recv[...].reshape(all_rows, LANES)
    values = v_recv[...].reshape(all_rows, LANES)
    key_index = lax.broadcasted_iota(jnp.int32, (1, all_rows), 1)
    valid = (key_index >= TEXT_SLOTS) | (key_index < text_len[0])

    def attend(piece):
        asked = jnp.concatenate([q_recv[4 * at + piece] for at in range(layers)], axis=0)
        lane = lax.broadcasted_iota(jnp.int32, asked.shape, 1)
        results = []
        for head in range(2):
            own = jnp.where((lane >= 64) == (head == 1), asked, jnp.zeros_like(asked))
            weights = jnp.where(valid, jnp.exp(dot_rows(own, keys)), 0.0)
            denominator = jnp.sum(weights, axis=1, keepdims=True)
            results.append(dot32(weights.astype(jnp.bfloat16), values) / denominator)
        every[me, piece] = jnp.where(lane < 64, results[0], results[1]).astype(jnp.bfloat16)

    def line(d):
        return (layer + layers - d) % layers * 4

    def z_copy(piece, d):
        target = (layer + d) % layers * 4 + in_layer
        block = every.at[me, piece]
        return remote(block, block, z_sem, piece * layers + d, (cfg, target))

    def x_copy(piece, d):
        block = every.at[line(d) + in_layer, piece]
        return remote(block, block, x_sem, piece * layers + d, (cfg, x_peer))

    def core_copy(piece, d):
        block = every.at[line(d) + in_layer, piece]
        return remote(block, block, core_sem, piece * layers + d, (cfg, core_peer))

    def cross_copy(piece, d):
        block = every.at[line(d) + x_peer % 4, piece]
        return remote(block, block, core_sem, (4 + piece) * layers + d, (cfg, core_peer))

    def give(piece):
        each(layers, lambda d: z_copy(piece, layers - d).start(), 1)
        x_copy(piece, 0).start()
        core_copy(piece, 0).start()

    def forward(piece):
        def from_line(d):
            z_copy(piece, d).wait_recv()
            x_copy(piece, d).start()
            core_copy(piece, d).start()
            x_copy(piece, d - 1).wait_recv()
            cross_copy(piece, d - 1).start()

        each(layers, from_line, 1)
        x_copy(piece, layers - 1).wait_recv()
        cross_copy(piece, layers - 1).start()

    def project(piece):
        each(layers, lambda d: core_copy(piece, d).wait_recv())
        each(layers, lambda d: cross_copy(piece, d).wait_recv())
        asked = jnp.concatenate([every[g, piece] for g in range(seq_count)], axis=1)
        shape = (layers, rows, own_width)
        own = dot_rows(asked, out_weight[...]).astype(jnp.bfloat16).reshape(shape)
        other = dot_rows(asked, partner_weight[...]).astype(jnp.bfloat16).reshape(shape)
        for at in range(layers):
            part[4 * at + piece, cfg] = own[at]
            part[4 * at + piece, 1 - cfg] = other[at]

        def hand_back(at):
            d = (4 * at + piece + seq_count - me) % seq_count

            @pl.when(d != 0)
            def _():
                back_copy(d).start()

        each(layers, hand_back)

    attend(0)
    give(0)
    attend(1)
    give(1)
    attend(2)
    give(2)
    forward(0)
    attend(3)
    give(3)
    forward(1)
    weight_copy.wait()
    forward(2)
    project(0)
    forward(3)
    project(1)
    project(2)
    project(3)
    back[me] = part[me]
    each(seq_count, lambda d: vec_copy(d).wait(), 1)
    for g in range(seq_count):
        gate_full[:, g * gate_width : (g + 1) * gate_width] = vec[g, :, 0:gate_width]
    for piece in range(4):
        each(layers, lambda d: z_copy(piece, d).wait_send(), 1)
        each(layers, lambda d: x_copy(piece, d).wait_send())
        each(layers, lambda d: core_copy(piece, d).wait_send())
        each(layers, lambda d: cross_copy(piece, d).wait_send())
    each(seq_count, lambda d: back_copy(d).wait(), 1)

    for half in range(2):
        for g in range(seq_count):
            first = (half * seq_count + g) * own_width
            total[:, first : first + own_width] = back[g, half].astype(jnp.float32)
    residual = hidden[...].astype(jnp.float32) + gate_full[...] * total[...]
    centred = residual - jnp.mean(residual, axis=1, keepdims=True)
    variance = jnp.mean(centred * centred, axis=1, keepdims=True)
    normed = centred * lax.rsqrt(variance + 1e-05)
    half_count = seq_count // 2
    shift = jnp.concatenate([vec[g, :, 256:] for g in range(half_count)], axis=1)
    scale = jnp.concatenate([vec[half_count + g, :, 256:] for g in range(half_count)], axis=1)
    normed = (normed * (1.0 + scale) + shift).astype(jnp.bfloat16)
    prediction = dot_rows(normed, proj_weight[...]) + proj_bias[...]
    width = prediction.shape[1] // 2
    is_cond = cfg == 0
    left, right = prediction[:, :width], prediction[:, width:]
    own = jnp.where(is_cond, left, right)
    pred_send[...] = jnp.where(is_cond, right, left)
    pred_copy = remote(pred_send, pred_recv, pair_sem, 1, (1 - cfg, me))
    pred_copy.start()
    pred_copy.wait()
    other = pred_recv[...]
    cond = jnp.where(is_cond, own, other)
    uncond = jnp.where(is_cond, other, own)
    guided = uncond + GUIDANCE * (cond - uncond)
    own_latent = jnp.where(is_cond, latent[:, :width], latent[:, width:])
    at = step_index[0]
    updated = solver_coef[0, at] * own_latent + solver_coef[1, at] * guided
    out_row = me * rows + lax.broadcasted_iota(jnp.int32, updated.shape, 0)
    out[...] = jnp.where(out_row >= TEXT_SLOTS, updated, 0.0)


def in_one_kernel(
    hidden, queries, key_proj, value_proj, norm_gain, norm_bias, positions, text_len, time_embed,
    gate_table, mod_table, out_weight, proj_weight, proj_bias, latent, solver_coef, step_index,
):
    seq_count = lax.axis_size("seq")
    rows = queries.shape[1]
    time_freq = 10000.0 ** (-2.0 * np.arange(8) / 16.0)
    space_freq = 10000.0 ** (-2.0 * np.arange(12) / 24.0)
    frequency = np.repeat(np.concatenate([time_freq, space_freq, space_freq]), 2)
    frequency = np.tile(frequency, 2).astype(np.float32)[None, :]
    own_width = out_weight.shape[1]
    model_width = hidden.shape[2]
    bf16, f32 = jnp.bfloat16, jnp.float32
    vec_width = 256 + mod_table.shape[1]
    out_width = latent.shape[1] // 2
    in_vmem = pl.BlockSpec(memory_space=pltpu.VMEM)
    in_hbm = pl.BlockSpec(memory_space=pltpu.HBM)
    in_smem = pl.BlockSpec(memory_space=pltpu.SMEM)

    large = [
        value_proj[0], key_proj[0], queries[0], gate_table.T, mod_table, out_weight.T, hidden[0],
        proj_weight.T, latent,
    ]

    def sems(count):
        return pltpu.SemaphoreType.DMA((2, count))

    return pl.pallas_call(
        functools.partial(step_kernel, seq_count),
        out_shape=jax.ShapeDtypeStruct((rows, out_width), f32),
        in_specs=[in_smem] * 3 + [in_vmem] * 6 + [in_hbm] * 9,
        out_specs=in_vmem,
        scratch_shapes=[pltpu.VMEM(value.shape, value.dtype) for value in large]
        + [
            pltpu.SemaphoreType.DMA((len(large),)),
            pltpu.VMEM((seq_count, rows, LANES), bf16),
            pltpu.VMEM((seq_count, rows, LANES), bf16),
            pltpu.VMEM((seq_count, rows, LANES), bf16),
            pltpu.VMEM((seq_count, rows, LANES), bf16),
            pltpu.VMEM((seq_count, rows, LANES), bf16),
            pltpu.VMEM((seq_count, rows, LANES), bf16),
            pltpu.VMEM((seq_count, 1, vec_width), f32),
            pltpu.VMEM(out_weight.shape[::-1], bf16),
            pltpu.VMEM((seq_count, 4, seq_count // 4 * rows, LANES), bf16),
            pltpu.VMEM((seq_count, 2, rows, own_width), bf16),
            pltpu.VMEM((seq_count, 2, rows, own_width), bf16),
            pltpu.VMEM((rows, model_width), f32),
            pltpu.VMEM((1, model_width), f32),
            pltpu.VMEM((rows, out_width), f32),
            pltpu.VMEM((rows, out_width), f32),
            sems(seq_count),
            sems(seq_count),
            sems(seq_count),
            sems(seq_count),
            sems(seq_count),
            sems(seq_count),
            sems(seq_count * 2),
            sems(seq_count),
            sems(2),
        ],
        compiler_params=pltpu.CompilerParams(
            collective_id=0, has_side_effects=True, vmem_limit_bytes=64 * 1024 * 1024 - 65536
        ),
        name="sampling_step",
    )(
        text_len, step_index, solver_coef,
        norm_gain, norm_bias, positions.T, frequency, time_embed[None, :], proj_bias[None, :],
        *large,
    )


def on_device(
    hidden,
    queries,
    key_proj,
    value_proj,
    norm_gain,
    norm_bias,
    positions,
    text_len,
    time_embed,
    gate_table,
    mod_table,
    out_weight,
    proj_weight,
    proj_bias,
    latent,
    solver_coef,
    step_index,
):
    seq_count = lax.axis_size("seq")
    seq_place = lax.axis_index("seq")
    local_rows = queries.shape[1]
    head_count = queries.shape[2] // 64
    head_group = max(head_count // seq_count, 1)
    row_split = max(seq_count // head_count, 1)
    part_rows = local_rows // row_split
    head_sets = head_count // head_group
    if head_group * 64 == LANES and seq_count % 4 == 0 and local_rows % 16 == 0:
        return in_one_kernel(
            hidden, queries, key_proj, value_proj, norm_gain, norm_bias, positions, text_len,
            time_embed, gate_table, mod_table, out_weight, proj_weight, proj_bias, latent,
            solver_coef, step_index,
        )
    row_index = seq_place * local_rows + jnp.arange(local_rows)
    is_video = row_index >= TEXT_SLOTS
    angles = rotary_angles(positions)
    rot_query = norm_rotate(queries[0], norm_gain[0], norm_bias[0], angles, is_video)
    rot_key = norm_rotate(key_proj[0], norm_gain[1], norm_bias[1], angles, is_video)
    query_send = rot_query.reshape(row_split, part_rows, head_sets, head_group, 64)
    query_send = query_send.transpose(2, 0, 1, 3, 4).reshape(seq_count, part_rows * head_group * 64)

    def spread(values):
        grouped = values.reshape(local_rows, head_sets, head_group * 64).transpose(1, 0, 2)
        widened = jnp.broadcast_to(
            grouped[:, None], (head_sets, row_split, local_rows, head_group * 64)
        )
        return widened.reshape(seq_count, local_rows * head_group * 64)

    key_send = spread(rot_key)
    value_send = spread(value_proj[0].reshape(local_rows, head_count, 64))
    query_recv, key_recv, value_recv = (
        lax.all_to_all(query_send, "seq", split_axis=0, concat_axis=0, tiled=True),
        lax.all_to_all(key_send, "seq", split_axis=0, concat_axis=0, tiled=True),
        lax.all_to_all(value_send, "seq", split_axis=0, concat_axis=0, tiled=True),
    )
    total_keys = seq_count * local_rows
    query_count = seq_count * part_rows
    query_all = query_recv.reshape(query_count, head_group, 64)
    key_index = jnp.arange(total_keys)
    key_valid = (key_index >= TEXT_SLOTS) | (key_index < text_len[0])
    block_keys = math.gcd(512, total_keys)
    block_count = total_keys // block_keys

    def key_step(state_pair, operands):
        numerator, denominator = state_pair
        key_block, value_block, valid_block = operands
        scores = (
            jnp.einsum("qgd,kgd->gqk", query_all, key_block, preferred_element_type=jnp.float32)
            * 0.125
        )
        weights = jnp.where(valid_block[None, None, :], jnp.exp(scores), 0.0)
        denominator = denominator + jnp.sum(weights, axis=2)
        numerator = numerator + jnp.einsum(
            "gqk,kgd->gqd",
            weights.astype(jnp.bfloat16),
            value_block,
            preferred_element_type=jnp.float32,
        )
        return ((numerator, denominator), None)

    start_state = (
        jnp.zeros((head_group, query_count, 64), jnp.float32),
        jnp.zeros((head_group, query_count), jnp.float32),
    )
    scanned = (
        key_recv.reshape(block_count, block_keys, head_group, 64),
        value_recv.reshape(block_count, block_keys, head_group, 64),
        key_valid.reshape(block_count, block_keys),
    )
    final_state, unused_out = lax.scan(key_step, start_state, scanned)
    attended = (final_state[0] / final_state[1][..., None]).astype(jnp.bfloat16)
    embed_act = jax.nn.silu(time_embed.astype(jnp.float32)).astype(jnp.bfloat16)[None, :]
    gate_own = jnp.dot(embed_act, gate_table, preferred_element_type=jnp.float32)
    mod_own = jnp.dot(embed_act, mod_table, preferred_element_type=jnp.float32)
    gate_width = gate_own.shape[1]
    vectors = lax.all_gather(jnp.concatenate([gate_own, mod_own], axis=1)[0], "seq", axis=0)
    gate_vec = vectors[:, :gate_width].reshape(-1)
    modulation = vectors[:, gate_width:].reshape(-1)
    if row_split == 1:
        projected = project_columns(attended, out_weight, seq_count, local_rows)
    else:
        projected = project_rows(attended, out_weight, seq_count, part_rows, row_split, head_sets)
    model_width = hidden.shape[2]
    residual = hidden[0].astype(jnp.float32) + gate_vec[None, :] * projected
    normed = (
        layer_norm(residual, 1e-05) * (1.0 + modulation[model_width:]) + modulation[:model_width]
    )
    normed = normed.astype(jnp.bfloat16)
    prediction = jnp.dot(normed, proj_weight, preferred_element_type=jnp.float32) + proj_bias
    cfg_place = lax.axis_index("cfg")
    own_width = prediction.shape[1] // 2
    own_pred = lax.dynamic_slice_in_dim(prediction, cfg_place * own_width, own_width, 1)
    sent_pred = lax.dynamic_slice_in_dim(prediction, (1 - cfg_place) * own_width, own_width, 1)
    partner = swapped(sent_pred, "cfg", 0)
    is_cond = cfg_place == 0
    cond_pred = jnp.where(is_cond, own_pred, partner)
    uncond_pred = jnp.where(is_cond, partner, own_pred)
    guided = uncond_pred + GUIDANCE * (cond_pred - uncond_pred)
    own_latent = lax.dynamic_slice_in_dim(latent, cfg_place * own_width, own_width, 1)
    step_coefs = lax.dynamic_index_in_dim(solver_coef, step_index[0], axis=1, keepdims=False)
    updated = step_coefs[0] * own_latent + step_coefs[1] * guided
    return jnp.where(is_video[:, None], updated, 0.0)


def solution(mesh):
    placed = (
        P("cfg", "seq", None),
        P("cfg", "seq", None),
        P("cfg", "seq", None),
        P("cfg", "seq", None),
        P(),
        P(),
        P(None, "seq"),
        P("cfg"),
        P(),
        P(None, "seq"),
        P(None, "seq"),
        P(None, ("cfg", "seq")),
        P(),
        P(),
        P("seq", None),
        P(),
        P(),
    )
    return jax.shard_map(
        on_device, mesh=mesh, in_specs=placed, out_specs=P("seq", "cfg"), check_vma=False
    )
```
